32 devices in a mesh: dp: 8 (over y, x, core), expert: 4 (over z).
Axes of the slice: x: 2, y: 2, z: 4, core: 2. Of those that a mesh axis runs over, the one named last changes fastest.
Arguments:
- frames: bfloat16 [16384, 1024], P(('dp', 'expert')), may hold values from -6 to 6
- lengths: int32 [64], P(('dp', 'expert')), may hold values from 64 to 256, as said below
- expert_ids: int32 [16384, 1], P(('dp', 'expert')), may hold values from 0 to 3; in each aligned block of 512 rows (0 to 511, 512 to 1023, ...) at most 144 rows name the same one
- conv_kernel: float32 [31, 1024], replicated, may hold values from -1 to 1
- conv_gain: float32 [1024], replicated, may hold values from 0.25 to 1.75
- ffn_gain: float32 [1024], replicated, may hold values from 0.25 to 1.75
- w_in: bfloat16 [4, 1024, 4096], P('expert'), may hold values from -0.1875 to 0.1875
- w_out: bfloat16 [4, 4096, 1024], P('expert'), may hold values from -0.09375 to 0.09375
- out_grad: bfloat16 [16384, 1024], P(('dp', 'expert')), may hold values from -6 to 6
Outputs:
- block_out: bfloat16 [16384, 1024], P(('dp', 'expert'))
- frames_grad: bfloat16 [16384, 1024], P(('dp', 'expert'))
- w_in_grad: float32 [4, 1024, 4096], P('expert', None, 'dp')
- w_out_grad: float32 [4, 4096, 1024], P('expert', 'dp')
- kernel_grad: float32 [31, 1024], replicated
- gain_grads: float32 [2, 1024], replicated
The draws below stay inside these ranges and needn't reach their ends.
Inputs may be any that keep to these rules, and one draw needn't show every extreme that they name: `expert_ids`: in the rows of one device (aligned blocks of 512 rows) no expert is named more than 144 times, a bound that some block reaches. `lengths`: all utterances of some device have 256 live frames.
All inputs are finite; a program needn't handle non-finite values.
Results may differ from the reference program's by a relative error of at most 0.0053.
Values may be sent and summed in bfloat16 or wider, within the bound.
A program may use at most 256 MiB of HBM per device.

```python
import math
import jax
import jax.numpy as jnp
import numpy as np
from jax import lax

D = 1024
FF = 4096
KS = 31
UTT_LEN = 256
UTT_DEV = 2
EXPERTS = 4
CAP = 144
UTTS = 64
FRAMES = 16384
N_DP = 8
N_EXPERT = 4


def draw_lengths(key, part):
    key_len, key_owner = jax.random.split(key)
    base_len = jax.random.randint(key_len, (UTTS,), UTT_LEN // 4, UTT_LEN + 1)
    owner_block = jax.random.randint(key_owner, (), 0, UTTS // UTT_DEV)
    block_of = jnp.arange(UTTS) // UTT_DEV
    return jnp.where(block_of == owner_block, UTT_LEN, base_len).astype(jnp.int32)


def block_scale(own_key, shape, cuts, low, top_value):
    gain = 1.0
    for dim, blocks in cuts:
        draws = jax.random.uniform(jax.random.fold_in(jax.random.fold_in(own_key, 6), dim), (blocks,), jnp.float32, low / len(cuts), top_value / len(cuts))
        gain = gain * jnp.repeat(jnp.exp(draws), shape[dim] // blocks).reshape((-1,) + (1,) * (len(shape) - 1 - dim))
    return gain


def shared_out(stream_key, own, number, rows, count, top, most, slope):
    ranking = jax.random.permutation(stream_key, count)
    crowded, usual = shares(count, rows * top, most, slope, True), shares(count, rows * top, most, slope, False)
    places = jnp.arange(count)

    def named(sizes, offset_by):
        used = int((sizes > 0).sum())
        fixed = max(1, used // 4)
        passed = fixed + (places - fixed + offset_by * (used - fixed)) % max(1, count - fixed)
        return jnp.zeros((count,), jnp.int32).at[ranking[jnp.where(places < fixed, places, passed)]].set(jnp.asarray(sizes, jnp.int32))

    sizes = jnp.where(number % 4 == 0, named(crowded, number // 4), named(usual, number - number // 4 - 1))
    mixed = jax.random.permutation(jax.random.fold_in(own, 3), count)
    donor, sink = mixed[0:count // 2 * 2:2], mixed[1:count // 2 * 2:2]
    room = jnp.minimum(sizes[donor] - 1, most - sizes[sink]) // 2
    room = jnp.where((donor == ranking[0]) | (sink == ranking[0]) | (sizes[sink] == 0), 0, jnp.maximum(room, 0))
    passed = jax.random.randint(jax.random.fold_in(own, 4), (count // 2,), 0, 1 << 20) % (room + 1)
    sizes = sizes.at[donor].add(-passed).at[sink].add(passed)
    items = jnp.searchsorted(jnp.cumsum(sizes), jnp.arange(rows * top), side="right").astype(jnp.int32)
    listing = items.reshape(top, rows).T
    listing = listing[jax.random.permutation(jax.random.fold_in(own, 1), rows)]
    offset_by = jax.random.randint(jax.random.fold_in(own, 2), (rows, 1), 0, top)
    return jnp.take_along_axis(listing, (jnp.arange(top)[None, :] + offset_by) % top, axis=1)


def shares(number_of, total, reach, slope, full):
    portions = [(1 << 20) // math.isqrt(grade ** slope) + 1 for grade in range(1, number_of + 1)]
    largest = reach if full else min(reach, max(-(-total // number_of), total * portions[0] // sum(portions)))
    least = 1 if total - largest >= number_of - 1 else 0
    given, surplus = [largest] + [least] * (number_of - 1), total - largest - least * (number_of - 1)
    while surplus > 0:
        movable = [i for i in range(1, number_of) if given[i] < largest] or [i for i in range(1, number_of) if given[i] < reach]
        whole, remaining = sum([portions[i] for i in movable]), surplus
        for i in movable:
            addition = min(reach - given[i], max(1, remaining * portions[i] // whole), surplus)
            given[i] = given[i] + addition
            surplus = surplus - addition
    return np.array(given)


def noise(key, extent, deviation, most, cuts=(), held_as=jnp.bfloat16):
    drawn = jax.random.normal(key, extent, jnp.float32) * deviation
    if len(cuts) > 0:
        drawn = block_scale(key, extent, cuts, -0.22, 0.18) * drawn
    return jnp.clip(drawn, min=-most, max=most).astype(held_as)


def setup_inputs(seed: int = 0) -> dict:
    key_of = jax.random.split(jax.random.key(seed), 10)
    frames = noise(key_of[0], (FRAMES, D), 1.0, 6.0, ((0, 32),))
    lengths = draw_lengths(jax.random.fold_in(key_of[9], 71), 0)
    expert_ids_keys = jax.random.split(jax.random.fold_in(key_of[2], 1), FRAMES // (UTT_DEV * UTT_LEN))
    expert_ids_turns = jax.random.permutation(jax.random.fold_in(key_of[2], 3), FRAMES // (UTT_DEV * UTT_LEN))
    expert_ids = jax.vmap(lambda own, number: shared_out(jax.random.fold_in(key_of[2], 2), own, number, UTT_DEV * UTT_LEN, EXPERTS, 1, CAP, 2))(expert_ids_keys, expert_ids_turns).reshape((FRAMES, 1))
    conv_kernel = noise(key_of[3], (KS, D), KS ** -0.5, 1.0, (), jnp.float32)
    conv_gain = jnp.clip(1.0 + 0.15 * jax.random.normal(key_of[4], (D,), jnp.float32), 0.25, 1.75)
    ffn_gain = jnp.clip(1.0 + 0.15 * jax.random.normal(key_of[5], (D,), jnp.float32), 0.25, 1.75)
    w_in = noise(key_of[6], (EXPERTS, D, FF), D ** -0.5, 0.1875, ((0, 4),))
    w_out = noise(key_of[7], (EXPERTS, FF, D), FF ** -0.5, 0.09375, ((0, 4),))
    out_grad = noise(key_of[8], (FRAMES, D), 1.0, 6.0, ((0, 32),))
    return dict(frames=frames, lengths=lengths, expert_ids=expert_ids, conv_kernel=conv_kernel, conv_gain=conv_gain, ffn_gain=ffn_gain, w_in=w_in, w_out=w_out, out_grad=out_grad)


def layer_norm(values, gain_vec):
    row_mean = lax.optimization_barrier(jnp.mean(values, axis=-1, keepdims=True))
    centered = values - row_mean
    row_var = lax.optimization_barrier(jnp.mean(centered * centered, axis=-1, keepdims=True))
    return centered * lax.rsqrt(row_var + 1e-05) * gain_vec

def conv_module(frames_f, live_mask, conv_kernel, conv_gain, ffn_gain):
    normed_conv = layer_norm(frames_f, conv_gain) * live_mask
    tap_count = conv_kernel.shape[0]
    half_span = (tap_count - 1) // 2
    utt_len = frames_f.shape[1]
    padded = jnp.pad(normed_conv, ((0, 0), (half_span, half_span), (0, 0)))
    conv_out = jnp.zeros_like(normed_conv)
    for tap_index in range(tap_count):
        conv_out = conv_out + conv_kernel[tap_index] * padded[:, tap_index:tap_index + utt_len]
    residual = frames_f + live_mask * jax.nn.silu(conv_out)
    return (residual, layer_norm(residual, ffn_gain))

def silu_slope(values):
    sig_val = jax.nn.sigmoid(values)
    return sig_val * (1.0 + values * (1.0 - sig_val))

def expert_pass(item):
    weights_in, weights_out, rows_in, rows_grad = item
    pre_act = jnp.dot(rows_in, weights_in, preferred_element_type=jnp.float32)
    hidden = jax.nn.silu(pre_act).astype(jnp.bfloat16)
    out_rows = jnp.dot(hidden, weights_out, preferred_element_type=jnp.float32).astype(jnp.bfloat16)
    hidden_grad = jnp.dot(rows_grad, weights_out.T, preferred_element_type=jnp.float32)
    pre_grad = (hidden_grad * silu_slope(pre_act)).astype(jnp.bfloat16)
    back_rows = jnp.dot(pre_grad, weights_in.T, preferred_element_type=jnp.float32).astype(jnp.bfloat16)
    grad_in = jnp.dot(rows_in.T, pre_grad, preferred_element_type=jnp.float32)
    grad_out = jnp.dot(hidden.T, rows_grad, preferred_element_type=jnp.float32)
    return (out_rows, back_rows, grad_in, grad_out)

def reference(frames, lengths, expert_ids, conv_kernel, conv_gain, ffn_gain, w_in, w_out, out_grad):
    block_count = UTTS // UTT_DEV
    live_mask = (jnp.arange(UTT_LEN, dtype=jnp.int32)[None, :] < lengths[:, None]).astype(jnp.float32)[:, :, None]
    frames_f = frames.astype(jnp.float32).reshape(block_count, UTT_DEV, UTT_LEN, D)
    mask_blocks = live_mask.reshape(block_count, UTT_DEV, UTT_LEN, 1)

    def forward_block(item):
        return conv_module(item[0], item[1], conv_kernel, conv_gain, ffn_gain)
    residual, normed = lax.map(forward_block, (frames_f, mask_blocks))
    residual = residual.reshape(FRAMES, D)
    expert_in = normed.reshape(FRAMES, D).astype(jnp.bfloat16)
    live_flat = live_mask.reshape(FRAMES) > 0.5
    slot_count = N_DP * N_EXPERT * CAP
    target = jnp.where(live_flat, expert_ids[:, 0], EXPERTS).astype(jnp.int32)
    one_hot = (target[:, None] == jnp.arange(EXPERTS, dtype=jnp.int32)[None, :]).astype(jnp.int32)
    rank_in = lax.optimization_barrier(jnp.sum((jnp.cumsum(one_hot, axis=0, dtype=jnp.int32) - 1) * one_hot, axis=1)).astype(jnp.int32)
    dest_slot = jnp.where(live_flat, target * slot_count + rank_in, EXPERTS * slot_count).astype(jnp.int32)
    routed_grad = jnp.where(live_flat[:, None], out_grad, jnp.zeros_like(out_grad))
    buffer_in = jnp.zeros((EXPERTS * slot_count, D), jnp.bfloat16).at[dest_slot].set(expert_in, mode='drop')
    buffer_grad = jnp.zeros((EXPERTS * slot_count, D), jnp.bfloat16).at[dest_slot].set(routed_grad, mode='drop')
    outs_all, backs_all, w_in_grad, w_out_grad = lax.map(expert_pass, (w_in, w_out, buffer_in.reshape(EXPERTS, slot_count, D), buffer_grad.reshape(EXPERTS, slot_count, D)))
    safe_slot = jnp.minimum(dest_slot, EXPERTS * slot_count - 1).astype(jnp.int32)
    zero_rows = jnp.zeros((FRAMES, D), jnp.float32)
    expert_out = jnp.where(live_flat[:, None], outs_all.reshape(EXPERTS * slot_count, D)[safe_slot].astype(jnp.float32), zero_rows)
    expert_back = jnp.where(live_flat[:, None], backs_all.reshape(EXPERTS * slot_count, D)[safe_slot].astype(jnp.float32), zero_rows)
    block_out = (residual + expert_out).astype(jnp.bfloat16)
    grad_blocks = out_grad.astype(jnp.float32).reshape(block_count, UTT_DEV, UTT_LEN, D)
    back_blocks = expert_back.reshape(block_count, UTT_DEV, UTT_LEN, D)

    def backward_block(item):
        block_frames, block_mask, block_grad, block_back = item

        def local_map(frames_in, kernel_in, gain_conv, gain_ffn):
            return conv_module(frames_in, block_mask, kernel_in, gain_conv, gain_ffn)
        unused_out, pull_back = jax.vjp(local_map, block_frames, conv_kernel, conv_gain, ffn_gain)
        return pull_back((block_grad, block_back))
    frames_grad, kernel_parts, conv_parts, ffn_parts = lax.map(backward_block, (frames_f, mask_blocks, grad_blocks, back_blocks))
    kernel_grad = lax.optimization_barrier(jnp.sum(kernel_parts, axis=0))
    gain_grads = jnp.stack([lax.optimization_barrier(jnp.sum(conv_parts, axis=0)), lax.optimization_barrier(jnp.sum(ffn_parts, axis=0))])
    return (block_out, frames_grad.reshape(FRAMES, D).astype(jnp.bfloat16), w_in_grad, w_out_grad, kernel_grad, gain_grads)
```

```python
import jax
import jax.numpy as jnp
from jax import lax
from jax.experimental import pallas as pl
from jax.experimental.pallas import tpu as pltpu
from jax.sharding import PartitionSpec as P

LANES = 128
EDGE = 16
ROWS = 32
F32 = jnp.float32
BF16 = jnp.bfloat16


def lane_slice(index):
    return pl.ds(pl.multiple_of(index * LANES, LANES), LANES)


def row_slice(start, count):
    return pl.ds(pl.multiple_of(start, ROWS), count)


def centred(values):
    row_mean = jnp.mean(values, axis=-1, keepdims=True)
    shifted = values - row_mean
    row_var = jnp.mean(shifted * shifted, axis=-1, keepdims=True)
    return shifted, lax.rsqrt(row_var + 1e-05)


def live_rows(start, count, length):
    return ((start + lax.broadcasted_iota(jnp.int32, (count, 1), 0)) < length).astype(F32)


def clear_edges(padded_ref, utt_len):
    zeros = jnp.zeros((padded_ref.shape[0], EDGE, LANES), F32)
    padded_ref[:, 0:EDGE, :] = zeros
    padded_ref[:, EDGE + utt_len :, :] = zeros


def scatter_lanes(padded_ref, start, count, values):
    for chunk in range(padded_ref.shape[0]):
        padded_ref[chunk, pl.ds(pl.multiple_of(start + EDGE, EDGE), count), :] = values[
            :, chunk * LANES : (chunk + 1) * LANES
        ]


def conv_forward_kernel(len_ref, x_ref, taps_ref, gain_ref, ffn_ref, res_ref, conv_ref, in_ref, pad_ref):
    length = len_ref[pl.program_id(0)]
    utt_len, width = x_ref.shape
    tap_count = taps_ref.shape[0]
    shift = EDGE - (tap_count - 1) // 2
    chunks = width // LANES
    clear_edges(pad_ref, utt_len)

    @pl.loop(0, utt_len // ROWS)
    def _(step):
        start = step * ROWS
        shifted, scale = centred(x_ref[row_slice(start, ROWS), :].astype(F32))
        normed = shifted * scale * gain_ref[...] * live_rows(start, ROWS, length)
        scatter_lanes(pad_ref, start, ROWS, normed)

    block = 64

    @pl.loop(0, chunks)
    def _(chunk):
        lanes = lane_slice(chunk)

        @pl.loop(0, utt_len // block)
        def _(step):
            start = step * block
            total = jnp.zeros((block, LANES), F32)
            for tap in range(tap_count):
                total = total + taps_ref[tap : tap + 1, lanes] * pad_ref[chunk, pl.ds(start + tap + shift, block), :]
            rows = row_slice(start, block)
            conv_ref[rows, lanes] = total
            silu = total * (1.0 / (1.0 + jnp.exp(-total)))
            res_ref[rows, lanes] = x_ref[rows, lanes].astype(F32) + live_rows(start, block, length) * silu

    @pl.loop(0, utt_len // ROWS)
    def _(step):
        rows = row_slice(step * ROWS, ROWS)
        shifted, scale = centred(res_ref[rows, :])
        in_ref[rows, :] = (shifted * scale * ffn_ref[...]).astype(BF16)


def fold_rows(values):
    return jnp.sum(values.reshape(values.shape[0] // 8, 8, values.shape[1]), axis=0)


def conv_backward_kernel(
    len_ref, x_ref, taps_ref, gain_ref, ffn_ref, res_ref, conv_ref, back_ref, grad_ref,
    out_ref, sums_ref, pad_ref, dpad_ref, dres_ref, dnorm_ref, gains_ref,
):
    utt = pl.program_id(0)
    length = len_ref[utt]
    utt_len, width = x_ref.shape
    tap_count = taps_ref.shape[0]
    half = (tap_count - 1) // 2
    chunks = width // LANES
    clear_edges(pad_ref, utt_len)
    clear_edges(dpad_ref, utt_len)

    @pl.when(utt == 0)
    def _():
        sums_ref[...] = jnp.zeros_like(sums_ref)
        gains_ref[...] = jnp.zeros_like(gains_ref)

    @pl.loop(0, utt_len // ROWS)
    def _(step):
        start = step * ROWS
        rows = row_slice(start, ROWS)
        live = live_rows(start, ROWS, length)
        shifted, scale = centred(x_ref[rows, :].astype(F32))
        scatter_lanes(pad_ref, start, ROWS, shifted * scale * gain_ref[...] * live)

    @pl.loop(0, utt_len // ROWS)
    def _(step):
        start = step * ROWS
        rows = row_slice(start, ROWS)
        live = live_rows(start, ROWS, length)
        shifted, scale = centred(res_ref[rows, :])
        unit = shifted * scale
        back = back_ref[rows, :].astype(F32)
        gains_ref[1] += fold_rows(back * unit)
        scaled = back * ffn_ref[...]
        mean_scaled = jnp.mean(scaled, axis=-1, keepdims=True)
        mean_product = jnp.mean(scaled * unit, axis=-1, keepdims=True)
        dres = grad_ref[rows, :].astype(F32) + scale * (scaled - mean_scaled - unit * mean_product)
        dres_ref[rows, :] = dres
        conv = conv_ref[rows, :]
        sig = 1.0 / (1.0 + jnp.exp(-conv))
        scatter_lanes(dpad_ref, start, ROWS, dres * live * (sig * (1.0 + conv * (1.0 - sig))))

    block = 32

    @pl.loop(0, chunks)
    def _(chunk):
        lanes = lane_slice(chunk)

        @pl.loop(0, utt_len // block)
        def _(step):
            start = step * block
            total = jnp.zeros((block, LANES), F32)
            for tap in range(tap_count):
                offset = EDGE + half - tap
                total = total + taps_ref[tap : tap + 1, lanes] * dpad_ref[chunk, pl.ds(start + offset, block), :]
            dnorm_ref[row_slice(start, block), lanes] = total

        def add_taps(step, totals):
            start = step * 16
            totals = list(totals)
            for part in range(2):
                cot = dpad_ref[chunk, pl.ds(pl.multiple_of(start + EDGE + 8 * part, 8), 8), :]
                for tap in range(tap_count):
                    offset = EDGE - half + tap + 8 * part
                    totals[tap] = totals[tap] + cot * pad_ref[chunk, pl.ds(start + offset, 8), :]
            return tuple(totals)

        totals = lax.fori_loop(
            0, utt_len // 16, add_taps, tuple(jnp.zeros((8, LANES), F32) for _ in range(tap_count))
        )
        for tap in range(tap_count):
            sums_ref[tap : tap + 1, lanes] += jnp.sum(totals[tap], axis=0, keepdims=True)

    @pl.loop(0, utt_len // ROWS)
    def _(step):
        start = step * ROWS
        rows = row_slice(start, ROWS)
        live = live_rows(start, ROWS, length)
        shifted, scale = centred(x_ref[rows, :].astype(F32))
        unit = shifted * scale
        dnorm = dnorm_ref[rows, :] * live
        gains_ref[0] += fold_rows(dnorm * unit)
        scaled = dnorm * gain_ref[...]
        mean_scaled = jnp.mean(scaled, axis=-1, keepdims=True)
        mean_product = jnp.mean(scaled * unit, axis=-1, keepdims=True)
        out_ref[rows, :] = (
            dres_ref[rows, :] + scale * (scaled - mean_scaled - unit * mean_product)
        ).astype(BF16)

    @pl.when(utt == pl.num_programs(0) - 1)
    def _():
        sums_ref[tap_count : tap_count + 1, :] = jnp.sum(gains_ref[0], axis=0, keepdims=True)
        sums_ref[tap_count + 1 : tap_count + 2, :] = jnp.sum(gains_ref[1], axis=0, keepdims=True)


def conv_specs(utt_len, width, tap_count):
    rows = pl.BlockSpec((utt_len, width), lambda utt: (utt, 0))
    vector = pl.BlockSpec((1, width), lambda utt: (0, 0))
    taps = pl.BlockSpec((tap_count, width), lambda utt: (0, 0))
    return rows, vector, taps


def conv_forward(frames, lengths, taps, gain, ffn):
    frame_count, width = frames.shape
    utt_count = lengths.shape[0]
    utt_len = frame_count // utt_count
    rows, vector, tap_spec = conv_specs(utt_len, width, taps.shape[0])
    return pl.pallas_call(
        conv_forward_kernel,
        grid=(utt_count,),
        out_shape=[
            jax.ShapeDtypeStruct((frame_count, width), F32),
            jax.ShapeDtypeStruct((frame_count, width), F32),
            jax.ShapeDtypeStruct((frame_count, width), BF16),
        ],
        in_specs=[pl.BlockSpec(memory_space=pltpu.SMEM), rows, tap_spec, vector, vector],
        out_specs=[rows, rows, rows],
        scratch_shapes=[pltpu.VMEM((width // LANES, utt_len + 2 * EDGE, LANES), F32)],
        compiler_params=pltpu.CompilerParams(vmem_limit_bytes=40 << 20),
        cost_estimate=pl.CostEstimate(flops=8 << 30, bytes_accessed=40 << 20, transcendentals=0),
        name="conv_forward",
    )(lengths, frames, taps, gain, ffn)


def conv_backward(frames, lengths, taps, gain, ffn, residual, conv_out, back, out_grad):
    frame_count, width = frames.shape
    utt_count = lengths.shape[0]
    utt_len = frame_count // utt_count
    tap_count = taps.shape[0]
    rows, vector, tap_spec = conv_specs(utt_len, width, tap_count)
    padded = pltpu.VMEM((width // LANES, utt_len + 2 * EDGE, LANES), F32)
    return pl.pallas_call(
        conv_backward_kernel,
        grid=(utt_count,),
        out_shape=[
            jax.ShapeDtypeStruct((frame_count, width), BF16),
            jax.ShapeDtypeStruct((tap_count + 2, width), F32),
        ],
        in_specs=[pl.BlockSpec(memory_space=pltpu.SMEM), rows, tap_spec, vector, vector, rows, rows, rows, rows],
        out_specs=[rows, pl.BlockSpec((tap_count + 2, width), lambda utt: (0, 0))],
        scratch_shapes=[
            padded,
            padded,
            pltpu.VMEM((utt_len, width), F32),
            pltpu.VMEM((utt_len, width), F32),
            pltpu.VMEM((2, 8, width), F32),
        ],
        compiler_params=pltpu.CompilerParams(vmem_limit_bytes=40 << 20),
        cost_estimate=pl.CostEstimate(flops=8 << 30, bytes_accessed=80 << 20, transcendentals=0),
        name="conv_backward",
    )(lengths, frames, taps, gain, ffn, residual, conv_out, back, out_grad)


def silu_slope(values):
    sig_val = jax.nn.sigmoid(values)
    return sig_val * (1.0 + values * (1.0 - sig_val))


def contract_rows(left_rows, right_rows):
    return lax.dot_general(left_rows, right_rows, (((0,), (0,)), ((), ())), preferred_element_type=F32)


def times_transpose(left_rows, matrix):
    return lax.dot_general(left_rows, matrix, (((1,), (1,)), ((), ())), preferred_element_type=F32)


def exchange(rows):
    return lax.all_to_all(rows, "expert", split_axis=0, concat_axis=0, tiled=True)


def shards(frames, lengths, expert_ids, conv_kernel, conv_gain, ffn_gain, w_in, w_out, out_grad):
    utt_count = lengths.shape[0]
    frame_count, width = frames.shape
    utt_len = frame_count // utt_count
    expert_count = lax.axis_size("expert")
    capacity = max(8, 8 * (9 * frame_count // (64 * expert_count)))
    slot_total = expert_count * capacity
    taps = conv_kernel.shape[0]
    gain = conv_gain.reshape(1, width)
    ffn = ffn_gain.reshape(1, width)

    live_flat = (jnp.arange(utt_len, dtype=jnp.int32)[None, :] < lengths[:, None]).reshape(frame_count)
    target = jnp.where(live_flat, expert_ids[:, 0], expert_count)
    one_hot = (target[:, None] == jnp.arange(expert_count, dtype=jnp.int32)[None, :]).astype(jnp.int32)
    rank_in = jnp.sum((jnp.cumsum(one_hot, axis=0, dtype=jnp.int32) - 1) * one_hot, axis=1)
    dest_slot = jnp.where(live_flat, target * capacity + rank_in, slot_total)
    placing = (jnp.arange(slot_total, dtype=jnp.int32)[:, None] == dest_slot[None, :]).astype(BF16)

    send_grad = jnp.dot(placing, out_grad, preferred_element_type=F32).astype(BF16)
    grad_rows = exchange(send_grad)
    residual, conv_out, expert_in = conv_forward(frames, lengths, conv_kernel, gain, ffn)
    send_in = jnp.dot(placing, expert_in, preferred_element_type=F32).astype(BF16)
    send_in, grad_rows = lax.optimization_barrier((send_in, grad_rows))
    routed_in = exchange(send_in)
    weights_in = w_in[0]
    weights_out = w_out[0]
    hidden_grad = times_transpose(grad_rows, weights_out)
    pre_act = jnp.dot(routed_in, weights_in, preferred_element_type=F32)
    hidden = jax.nn.silu(pre_act).astype(BF16)
    pre_grad = (hidden_grad * silu_slope(pre_act)).astype(BF16)
    back_rows = times_transpose(pre_grad, weights_in).astype(BF16)
    ret_back = exchange(back_rows)
    pre_grad, back_rows = lax.optimization_barrier((pre_grad, back_rows))
    full_in = contract_rows(routed_in, pre_grad).astype(BF16)
    full_out = contract_rows(hidden, grad_rows).astype(BF16)
    grad_in = lax.psum_scatter(full_in, "dp", scatter_dimension=1, tiled=True).astype(F32)
    grad_out = lax.psum_scatter(full_out, "dp", scatter_dimension=0, tiled=True).astype(F32)
    hidden, full_in, full_out, ret_back = lax.optimization_barrier((hidden, full_in, full_out, ret_back))
    out_rows = jnp.dot(hidden, weights_out, preferred_element_type=F32).astype(BF16)
    ret_out = exchange(out_rows)

    expert_back = contract_rows(placing, ret_back).astype(BF16)
    frames_grad, sums = conv_backward(
        frames, lengths, conv_kernel, gain, ffn, residual, conv_out, expert_back, out_grad
    )
    block_out = (residual + contract_rows(placing, ret_out)).astype(BF16)
    sums = lax.psum(sums, ("dp", "expert"))
    return (block_out, frames_grad, grad_in[None], grad_out[None], sums[:taps], sums[taps:])


def solution(mesh):
    return jax.shard_map(
        shards,
        mesh=mesh,
        in_specs=(
            P(("dp", "expert"), None),
            P(("dp", "expert")),
            P(("dp", "expert"), None),
            P(),
            P(),
            P(),
            P("expert", None, None),
            P("expert", None, None),
            P(("dp", "expert"), None),
        ),
        out_specs=(
            P(("dp", "expert"), None),
            P(("dp", "expert"), None),
            P("expert", None, "dp"),
            P("expert", "dp", None),
            P(),
            P(),
        ),
        check_vma=False,
    )
```

```python
import jax
import jax.numpy as jnp
from jax import lax
from jax.experimental import pallas as pl
from jax.experimental.pallas import tpu as pltpu
from jax.sharding import PartitionSpec as P

LANES = 128
EDGE = 16
ROWS = 32
F32 = jnp.float32
BF16 = jnp.bfloat16


def lane_slice(index):
    return pl.ds(pl.multiple_of(index * LANES, LANES), LANES)


def row_slice(start, count):
    return pl.ds(pl.multiple_of(start, ROWS), count)


def centred(values):
    row_mean = jnp.mean(values, axis=-1, keepdims=True)
    shifted = values - row_mean
    row_var = jnp.mean(shifted * shifted, axis=-1, keepdims=True)
    return shifted, lax.rsqrt(row_var + 1e-05)


def live_rows(start, count, length):
    return ((start + lax.broadcasted_iota(jnp.int32, (count, 1), 0)) < length).astype(F32)


def clear_edges(padded_ref, utt_len):
    zeros = jnp.zeros((padded_ref.shape[0], EDGE, LANES), F32)
    padded_ref[:, 0:EDGE, :] = zeros
    padded_ref[:, EDGE + utt_len :, :] = zeros


def scatter_lanes(padded_ref, start, count, values):
    for chunk in range(padded_ref.shape[0]):
        padded_ref[chunk, pl.ds(pl.multiple_of(start + EDGE, EDGE), count), :] = values[
            :, chunk * LANES : (chunk + 1) * LANES
        ]


def conv_forward_kernel(len_ref, x_ref, taps_ref, gain_ref, ffn_ref, res_ref, conv_ref, in_ref, pad_ref):
    length = len_ref[pl.program_id(0)]
    utt_len, width = x_ref.shape
    tap_count = taps_ref.shape[0]
    shift = EDGE - (tap_count - 1) // 2
    chunks = width // LANES
    clear_edges(pad_ref, utt_len)

    @pl.loop(0, utt_len // ROWS)
    def _(step):
        start = step * ROWS
        shifted, scale = centred(x_ref[row_slice(start, ROWS), :].astype(F32))
        normed = shifted * scale * gain_ref[...] * live_rows(start, ROWS, length)
        scatter_lanes(pad_ref, start, ROWS, normed)

    block = 64

    @pl.loop(0, chunks)
    def _(chunk):
        lanes = lane_slice(chunk)

        @pl.loop(0, utt_len // block)
        def _(step):
            start = step * block
            total = jnp.zeros((block, LANES), F32)
            for tap in range(tap_count):
                total = total + taps_ref[tap : tap + 1, lanes] * pad_ref[chunk, pl.ds(start + tap + shift, block), :]
            rows = row_slice(start, block)
            conv_ref[rows, lanes] = total
            silu = total * (1.0 / (1.0 + jnp.exp(-total)))
            res_ref[rows, lanes] = x_ref[rows, lanes].astype(F32) + live_rows(start, block, length) * silu

    @pl.loop(0, utt_len // ROWS)
    def _(step):
        rows = row_slice(step * ROWS, ROWS)
        shifted, scale = centred(res_ref[rows, :])
        in_ref[rows, :] = (shifted * scale * ffn_ref[...]).astype(BF16)


def fold_rows(values):
    return jnp.sum(values.reshape(values.shape[0] // 8, 8, values.shape[1]), axis=0)


def conv_backward_kernel(
    len_ref, x_ref, taps_ref, gain_ref, ffn_ref, res_ref, conv_ref, back_ref, grad_ref,
    out_ref, sums_ref, pad_ref, dpad_ref, dres_ref, dnorm_ref, gains_ref,
):
    utt = pl.program_id(0)
    length = len_ref[utt]
    utt_len, width = x_ref.shape
    tap_count = taps_ref.shape[0]
    half = (tap_count - 1) // 2
    chunks = width // LANES
    clear_edges(pad_ref, utt_len)
    clear_edges(dpad_ref, utt_len)

    @pl.when(utt == 0)
    def _():
        sums_ref[...] = jnp.zeros_like(sums_ref)
        gains_ref[...] = jnp.zeros_like(gains_ref)

    @pl.loop(0, utt_len // ROWS)
    def _(step):
        start = step * ROWS
        rows = row_slice(start, ROWS)
        live = live_rows(start, ROWS, length)
        shifted, scale = centred(x_ref[rows, :].astype(F32))
        scatter_lanes(pad_ref, start, ROWS, shifted * scale * gain_ref[...] * live)

    @pl.loop(0, utt_len // ROWS)
    def _(step):
        start = step * ROWS
        rows = row_slice(start, ROWS)
        live = live_rows(start, ROWS, length)
        shifted, scale = centred(res_ref[rows, :])
        unit = shifted * scale
        back = back_ref[rows, :].astype(F32)
        gains_ref[1] += fold_rows(back * unit)
        scaled = back * ffn_ref[...]
        mean_scaled = jnp.mean(scaled, axis=-1, keepdims=True)
        mean_product = jnp.mean(scaled * unit, axis=-1, keepdims=True)
        dres = grad_ref[rows, :].astype(F32) + scale * (scaled - mean_scaled - unit * mean_product)
        dres_ref[rows, :] = dres
        conv = conv_ref[rows, :]
        sig = 1.0 / (1.0 + jnp.exp(-conv))
        scatter_lanes(dpad_ref, start, ROWS, dres * live * (sig * (1.0 + conv * (1.0 - sig))))

    block = 32

    @pl.loop(0, chunks)
    def _(chunk):
        lanes = lane_slice(chunk)

        @pl.loop(0, utt_len // block)
        def _(step):
            start = step * block
            total = jnp.zeros((block, LANES), F32)
            for tap in range(tap_count):
                offset = EDGE + half - tap
                total = total + taps_ref[tap : tap + 1, lanes] * dpad_ref[chunk, pl.ds(start + offset, block), :]
            dnorm_ref[row_slice(start, block), lanes] = total

        def add_taps(step, totals):
            start = step * 16
            totals = list(totals)
            for part in range(2):
                cot = dpad_ref[chunk, pl.ds(pl.multiple_of(start + EDGE + 8 * part, 8), 8), :]
                for tap in range(tap_count):
                    offset = EDGE - half + tap + 8 * part
                    totals[tap] = totals[tap] + cot * pad_ref[chunk, pl.ds(start + offset, 8), :]
            return tuple(totals)

        totals = lax.fori_loop(
            0, utt_len // 16, add_taps, tuple(jnp.zeros((8, LANES), F32) for _ in range(tap_count))
        )
        for tap in range(tap_count):
            sums_ref[tap : tap + 1, lanes] += jnp.sum(totals[tap], axis=0, keepdims=True)

    @pl.loop(0, utt_len // ROWS)
    def _(step):
        start = step * ROWS
        rows = row_slice(start, ROWS)
        live = live_rows(start, ROWS, length)
        shifted, scale = centred(x_ref[rows, :].astype(F32))
        unit = shifted * scale
        dnorm = dnorm_ref[rows, :] * live
        gains_ref[0] += fold_rows(dnorm * unit)
        scaled = dnorm * gain_ref[...]
        mean_scaled = jnp.mean(scaled, axis=-1, keepdims=True)
        mean_product = jnp.mean(scaled * unit, axis=-1, keepdims=True)
        out_ref[rows, :] = (
            dres_ref[rows, :] + scale * (scaled - mean_scaled - unit * mean_product)
        ).astype(BF16)

    @pl.when(utt == pl.num_programs(0) - 1)
    def _():
        sums_ref[tap_count : tap_count + 1, :] = jnp.sum(gains_ref[0], axis=0, keepdims=True)
        sums_ref[tap_count + 1 : tap_count + 2, :] = jnp.sum(gains_ref[1], axis=0, keepdims=True)


def conv_specs(utt_len, width, tap_count):
    rows = pl.BlockSpec((utt_len, width), lambda utt: (utt, 0))
    vector = pl.BlockSpec((1, width), lambda utt: (0, 0))
    taps = pl.BlockSpec((tap_count, width), lambda utt: (0, 0))
    return rows, vector, taps


def conv_forward(frames, lengths, taps, gain, ffn):
    frame_count, width = frames.shape
    utt_count = lengths.shape[0]
    utt_len = frame_count // utt_count
    rows, vector, tap_spec = conv_specs(utt_len, width, taps.shape[0])
    return pl.pallas_call(
        conv_forward_kernel,
        grid=(utt_count,),
        out_shape=[
            jax.ShapeDtypeStruct((frame_count, width), F32),
            jax.ShapeDtypeStruct((frame_count, width), F32),
            jax.ShapeDtypeStruct((frame_count, width), BF16),
        ],
        in_specs=[pl.BlockSpec(memory_space=pltpu.SMEM), rows, tap_spec, vector, vector],
        out_specs=[rows, rows, rows],
        scratch_shapes=[pltpu.VMEM((width // LANES, utt_len + 2 * EDGE, LANES), F32)],
        compiler_params=pltpu.CompilerParams(vmem_limit_bytes=40 << 20),
        cost_estimate=pl.CostEstimate(flops=8 << 30, bytes_accessed=40 << 20, transcendentals=0),
        name="conv_forward",
    )(lengths, frames, taps, gain, ffn)


def conv_backward(frames, lengths, taps, gain, ffn, residual, conv_out, back, out_grad):
    frame_count, width = frames.shape
    utt_count = lengths.shape[0]
    utt_len = frame_count // utt_count
    tap_count = taps.shape[0]
    rows, vector, tap_spec = conv_specs(utt_len, width, tap_count)
    padded = pltpu.VMEM((width // LANES, utt_len + 2 * EDGE, LANES), F32)
    return pl.pallas_call(
        conv_backward_kernel,
        grid=(utt_count,),
        out_shape=[
            jax.ShapeDtypeStruct((frame_count, width), BF16),
            jax.ShapeDtypeStruct((tap_count + 2, width), F32),
        ],
        in_specs=[pl.BlockSpec(memory_space=pltpu.SMEM), rows, tap_spec, vector, vector, rows, rows, rows, rows],
        out_specs=[rows, pl.BlockSpec((tap_count + 2, width), lambda utt: (0, 0))],
        scratch_shapes=[
            padded,
            padded,
            pltpu.VMEM((utt_len, width), F32),
            pltpu.VMEM((utt_len, width), F32),
            pltpu.VMEM((2, 8, width), F32),
        ],
        compiler_params=pltpu.CompilerParams(vmem_limit_bytes=40 << 20),
        cost_estimate=pl.CostEstimate(flops=8 << 30, bytes_accessed=80 << 20, transcendentals=0),
        name="conv_backward",
    )(lengths, frames, taps, gain, ffn, residual, conv_out, back, out_grad)


def silu_slope(values):
    sig_val = jax.nn.sigmoid(values)
    return sig_val * (1.0 + values * (1.0 - sig_val))


def contract_rows(left_rows, right_rows):
    return lax.dot_general(left_rows, right_rows, (((0,), (0,)), ((), ())), preferred_element_type=F32)


def times_transpose(left_rows, matrix):
    return lax.dot_general(left_rows, matrix, (((1,), (1,)), ((), ())), preferred_element_type=F32)


def exchange(rows):
    return lax.all_to_all(rows, "expert", split_axis=0, concat_axis=0, tiled=True)


def column_part(matrix, place, part):
    return lax.dynamic_slice_in_dim(matrix, place * part, part, axis=1)


def sum_over_dp(part_of, flip):
    count = lax.axis_size("dp")
    me = lax.axis_index("dp")
    steps = [1 << bit for bit in range(count.bit_length() - 1)]
    if flip:
        steps = steps[:1] + steps[:0:-1]
    order = sorted(range(count), key=lambda piece: -(piece & 1))
    pieces = {piece: part_of(me ^ piece) for piece in order}
    for bit in steps:
        pairs = [(device, device ^ bit) for device in range(count)]
        arrived = {
            piece ^ bit: lax.ppermute(pieces[piece].astype(BF16), "dp", pairs) for piece in pieces if piece & bit
        }
        pieces = {piece: pieces[piece] + arrived[piece].astype(F32) for piece in arrived}
    return pieces[0]


def shards(frames, lengths, expert_ids, conv_kernel, conv_gain, ffn_gain, w_in, w_out, out_grad):
    utt_count = lengths.shape[0]
    frame_count, width = frames.shape
    utt_len = frame_count // utt_count
    expert_count = lax.axis_size("expert")
    capacity = max(8, 8 * (9 * frame_count // (64 * expert_count)))
    slot_total = expert_count * capacity
    taps = conv_kernel.shape[0]
    gain = conv_gain.reshape(1, width)
    ffn = ffn_gain.reshape(1, width)

    live_flat = (jnp.arange(utt_len, dtype=jnp.int32)[None, :] < lengths[:, None]).reshape(frame_count)
    target = jnp.where(live_flat, expert_ids[:, 0], expert_count)
    one_hot = (target[:, None] == jnp.arange(expert_count, dtype=jnp.int32)[None, :]).astype(jnp.int32)
    rank_in = jnp.sum((jnp.cumsum(one_hot, axis=0, dtype=jnp.int32) - 1) * one_hot, axis=1)
    dest_slot = jnp.where(live_flat, target * capacity + rank_in, slot_total)
    placing = (jnp.arange(slot_total, dtype=jnp.int32)[:, None] == dest_slot[None, :]).astype(BF16)

    send_grad = jnp.dot(placing, out_grad, preferred_element_type=F32).astype(BF16)
    grad_rows = exchange(send_grad)
    residual, conv_out, expert_in = conv_forward(frames, lengths, conv_kernel, gain, ffn)
    send_in = jnp.dot(placing, expert_in, preferred_element_type=F32).astype(BF16)
    send_in, grad_rows = lax.optimization_barrier((send_in, grad_rows))
    routed_in = exchange(send_in)
    weights_in = w_in[0]
    weights_out = w_out[0]
    hidden_grad = times_transpose(grad_rows, weights_out)
    pre_act = jnp.dot(routed_in, weights_in, preferred_element_type=F32)
    hidden = jax.nn.silu(pre_act).astype(BF16)
    pre_grad = (hidden_grad * silu_slope(pre_act)).astype(BF16)
    back_rows = times_transpose(pre_grad, weights_in).astype(BF16)
    ret_back = exchange(back_rows)
    pre_grad, back_rows = lax.optimization_barrier((pre_grad, back_rows))
    part = w_in.shape[2] // lax.axis_size("dp")
    grad_in = sum_over_dp(lambda place: contract_rows(routed_in, column_part(pre_grad, place, part)), False)
    grad_out = sum_over_dp(lambda place: contract_rows(column_part(hidden, place, part), grad_rows), True)
    out_rows = jnp.dot(hidden, weights_out, preferred_element_type=F32).astype(BF16)
    ret_out = exchange(out_rows)

    expert_back = contract_rows(placing, ret_back).astype(BF16)
    frames_grad, sums = conv_backward(
        frames, lengths, conv_kernel, gain, ffn, residual, conv_out, expert_back, out_grad
    )
    block_out = (residual + contract_rows(placing, ret_out)).astype(BF16)
    sums = lax.psum(sums, ("dp", "expert"))
    return (block_out, frames_grad, grad_in[None], grad_out[None], sums[:taps], sums[taps:])


def solution(mesh):
    return jax.shard_map(
        shards,
        mesh=mesh,
        in_specs=(
            P(("dp", "expert"), None),
            P(("dp", "expert")),
            P(("dp", "expert"), None),
            P(),
            P(),
            P(),
            P("expert", None, None),
            P("expert", None, None),
            P(("dp", "expert"), None),
        ),
        out_specs=(
            P(("dp", "expert"), None),
            P(("dp", "expert"), None),
            P("expert", None, "dp"),
            P("expert", "dp", None),
            P(),
            P(),
        ),
        check_vma=False,
    )
```

```python
import jax
import jax.numpy as jnp
from jax import lax
from jax.experimental import pallas as pl
from jax.experimental.pallas import tpu as pltpu
from jax.sharding import PartitionSpec as P

LANES = 128
EDGE = 16
ROWS = 32
F32 = jnp.float32
BF16 = jnp.bfloat16


def lane_slice(index):
    return pl.ds(pl.multiple_of(index * LANES, LANES), LANES)


def row_slice(start, count):
    return pl.ds(pl.multiple_of(start, ROWS), count)


def centred(values):
    row_mean = jnp.mean(values, axis=-1, keepdims=True)
    shifted = values - row_mean
    row_var = jnp.mean(shifted * shifted, axis=-1, keepdims=True)
    return shifted, lax.rsqrt(row_var + 1e-05)


def live_rows(start, count, length):
    return ((start + lax.broadcasted_iota(jnp.int32, (count, 1), 0)) < length).astype(F32)


def clear_edges(padded_ref, utt_len):
    zeros = jnp.zeros((padded_ref.shape[0], EDGE, LANES), F32)
    padded_ref[:, 0:EDGE, :] = zeros
    padded_ref[:, EDGE + utt_len :, :] = zeros


def scatter_lanes(padded_ref, start, count, values):
    for chunk in range(padded_ref.shape[0]):
        padded_ref[chunk, pl.ds(pl.multiple_of(start + EDGE, EDGE), count), :] = values[
            :, chunk * LANES : (chunk + 1) * LANES
        ]


def conv_forward_kernel(len_ref, x_ref, taps_ref, gain_ref, ffn_ref, res_ref, conv_ref, in_ref, pad_ref):
    length = len_ref[pl.program_id(0)]
    utt_len, width = x_ref.shape
    tap_count = taps_ref.shape[0]
    shift = EDGE - (tap_count - 1) // 2
    chunks = width // LANES
    clear_edges(pad_ref, utt_len)

    @pl.loop(0, utt_len // ROWS)
    def _(step):
        start = step * ROWS
        shifted, scale = centred(x_ref[row_slice(start, ROWS), :].astype(F32))
        normed = shifted * scale * gain_ref[...] * live_rows(start, ROWS, length)
        scatter_lanes(pad_ref, start, ROWS, normed)

    block = 64

    @pl.loop(0, chunks)
    def _(chunk):
        lanes = lane_slice(chunk)

        @pl.loop(0, utt_len // block)
        def _(step):
            start = step * block
            total = jnp.zeros((block, LANES), F32)
            for tap in range(tap_count):
                total = total + taps_ref[tap : tap + 1, lanes] * pad_ref[chunk, pl.ds(start + tap + shift, block), :]
            rows = row_slice(start, block)
            conv_ref[rows, lanes] = total
            silu = total * (1.0 / (1.0 + jnp.exp(-total)))
            res_ref[rows, lanes] = x_ref[rows, lanes].astype(F32) + live_rows(start, block, length) * silu

    @pl.loop(0, utt_len // ROWS)
    def _(step):
        rows = row_slice(step * ROWS, ROWS)
        shifted, scale = centred(res_ref[rows, :])
        in_ref[rows, :] = (shifted * scale * ffn_ref[...]).astype(BF16)


def fold_rows(values):
    return jnp.sum(values.reshape(values.shape[0] // 8, 8, values.shape[1]), axis=0)


def conv_backward_kernel(
    len_ref, x_ref, taps_ref, gain_ref, ffn_ref, res_ref, conv_ref, back_ref, grad_ref,
    out_ref, sums_ref, pad_ref, dpad_ref, dres_ref, dnorm_ref, gains_ref,
):
    utt = pl.program_id(0)
    length = len_ref[utt]
    utt_len, width = x_ref.shape
    tap_count = taps_ref.shape[0]
    half = (tap_count - 1) // 2
    chunks = width // LANES
    clear_edges(pad_ref, utt_len)
    clear_edges(dpad_ref, utt_len)

    @pl.when(utt == 0)
    def _():
        sums_ref[...] = jnp.zeros_like(sums_ref)
        gains_ref[...] = jnp.zeros_like(gains_ref)

    @pl.loop(0, utt_len // ROWS)
    def _(step):
        start = step * ROWS
        rows = row_slice(start, ROWS)
        live = live_rows(start, ROWS, length)
        shifted, scale = centred(x_ref[rows, :].astype(F32))
        scatter_lanes(pad_ref, start, ROWS, shifted * scale * gain_ref[...] * live)

    @pl.loop(0, utt_len // ROWS)
    def _(step):
        start = step * ROWS
        rows = row_slice(start, ROWS)
        live = live_rows(start, ROWS, length)
        shifted, scale = centred(res_ref[rows, :])
        unit = shifted * scale
        back = back_ref[rows, :].astype(F32)
        gains_ref[1] += fold_rows(back * unit)
        scaled = back * ffn_ref[...]
        mean_scaled = jnp.mean(scaled, axis=-1, keepdims=True)
        mean_product = jnp.mean(scaled * unit, axis=-1, keepdims=True)
        dres = grad_ref[rows, :].astype(F32) + scale * (scaled - mean_scaled - unit * mean_product)
        dres_ref[rows, :] = dres
        conv = conv_ref[rows, :]
        sig = 1.0 / (1.0 + jnp.exp(-conv))
        scatter_lanes(dpad_ref, start, ROWS, dres * live * (sig * (1.0 + conv * (1.0 - sig))))

    block = 32

    @pl.loop(0, chunks)
    def _(chunk):
        lanes = lane_slice(chunk)

        @pl.loop(0, utt_len // block)
        def _(step):
            start = step * block
            total = jnp.zeros((block, LANES), F32)
            for tap in range(tap_count):
                offset = EDGE + half - tap
                total = total + taps_ref[tap : tap + 1, lanes] * dpad_ref[chunk, pl.ds(start + offset, block), :]
            dnorm_ref[row_slice(start, block), lanes] = total

        def add_taps(step, totals):
            start = step * 16
            totals = list(totals)
            for part in range(2):
                cot = dpad_ref[chunk, pl.ds(pl.multiple_of(start + EDGE + 8 * part, 8), 8), :]
                for tap in range(tap_count):
                    offset = EDGE - half + tap + 8 * part
                    totals[tap] = totals[tap] + cot * pad_ref[chunk, pl.ds(start + offset, 8), :]
            return tuple(totals)

        totals = lax.fori_loop(
            0, utt_len // 16, add_taps, tuple(jnp.zeros((8, LANES), F32) for _ in range(tap_count))
        )
        for tap in range(tap_count):
            sums_ref[tap : tap + 1, lanes] += jnp.sum(totals[tap], axis=0, keepdims=True)

    @pl.loop(0, utt_len // ROWS)
    def _(step):
        start = step * ROWS
        rows = row_slice(start, ROWS)
        live = live_rows(start, ROWS, length)
        shifted, scale = centred(x_ref[rows, :].astype(F32))
        unit = shifted * scale
        dnorm = dnorm_ref[rows, :] * live
        gains_ref[0] += fold_rows(dnorm * unit)
        scaled = dnorm * gain_ref[...]
        mean_scaled = jnp.mean(scaled, axis=-1, keepdims=True)
        mean_product = jnp.mean(scaled * unit, axis=-1, keepdims=True)
        out_ref[rows, :] = (
            dres_ref[rows, :] + scale * (scaled - mean_scaled - unit * mean_product)
        ).astype(BF16)

    @pl.when(utt == pl.num_programs(0) - 1)
    def _():
        sums_ref[tap_count : tap_count + 1, :] = jnp.sum(gains_ref[0], axis=0, keepdims=True)
        sums_ref[tap_count + 1 : tap_count + 2, :] = jnp.sum(gains_ref[1], axis=0, keepdims=True)


def conv_specs(utt_len, width, tap_count):
    rows = pl.BlockSpec((utt_len, width), lambda utt: (utt, 0))
    vector = pl.BlockSpec((1, width), lambda utt: (0, 0))
    taps = pl.BlockSpec((tap_count, width), lambda utt: (0, 0))
    return rows, vector, taps


def conv_forward(frames, lengths, taps, gain, ffn):
    frame_count, width = frames.shape
    utt_count = lengths.shape[0]
    utt_len = frame_count // utt_count
    rows, vector, tap_spec = conv_specs(utt_len, width, taps.shape[0])
    return pl.pallas_call(
        conv_forward_kernel,
        grid=(utt_count,),
        out_shape=[
            jax.ShapeDtypeStruct((frame_count, width), F32),
            jax.ShapeDtypeStruct((frame_count, width), F32),
            jax.ShapeDtypeStruct((frame_count, width), BF16),
        ],
        in_specs=[pl.BlockSpec(memory_space=pltpu.SMEM), rows, tap_spec, vector, vector],
        out_specs=[rows, rows, rows],
        scratch_shapes=[pltpu.VMEM((width // LANES, utt_len + 2 * EDGE, LANES), F32)],
        compiler_params=pltpu.CompilerParams(vmem_limit_bytes=40 << 20),
        cost_estimate=pl.CostEstimate(flops=8 << 30, bytes_accessed=40 << 20, transcendentals=0),
        name="conv_forward",
    )(lengths, frames, taps, gain, ffn)


def conv_backward(frames, lengths, taps, gain, ffn, residual, conv_out, back, out_grad):
    frame_count, width = frames.shape
    utt_count = lengths.shape[0]
    utt_len = frame_count // utt_count
    tap_count = taps.shape[0]
    rows, vector, tap_spec = conv_specs(utt_len, width, tap_count)
    padded = pltpu.VMEM((width // LANES, utt_len + 2 * EDGE, LANES), F32)
    return pl.pallas_call(
        conv_backward_kernel,
        grid=(utt_count,),
        out_shape=[
            jax.ShapeDtypeStruct((frame_count, width), BF16),
            jax.ShapeDtypeStruct((tap_count + 2, width), F32),
        ],
        in_specs=[pl.BlockSpec(memory_space=pltpu.SMEM), rows, tap_spec, vector, vector, rows, rows, rows, rows],
        out_specs=[rows, pl.BlockSpec((tap_count + 2, width), lambda utt: (0, 0))],
        scratch_shapes=[
            padded,
            padded,
            pltpu.VMEM((utt_len, width), F32),
            pltpu.VMEM((utt_len, width), F32),
            pltpu.VMEM((2, 8, width), F32),
        ],
        compiler_params=pltpu.CompilerParams(vmem_limit_bytes=40 << 20),
        cost_estimate=pl.CostEstimate(flops=8 << 30, bytes_accessed=80 << 20, transcendentals=0),
        name="conv_backward",
    )(lengths, frames, taps, gain, ffn, residual, conv_out, back, out_grad)


def silu_slope(values):
    sig_val = jax.nn.sigmoid(values)
    return sig_val * (1.0 + values * (1.0 - sig_val))


def contract_rows(left_rows, right_rows):
    return lax.dot_general(left_rows, right_rows, (((0,), (0,)), ((), ())), preferred_element_type=F32)


def times_transpose(left_rows, matrix):
    return lax.dot_general(left_rows, matrix, (((1,), (1,)), ((), ())), preferred_element_type=F32)


def exchange(rows):
    return lax.all_to_all(rows, "expert", split_axis=0, concat_axis=0, tiled=True)


def column_part(matrix, place, part):
    return lax.dynamic_slice_in_dim(matrix, place * part, part, axis=1)


def sum_over_dp(part_of, flip):
    count = lax.axis_size("dp")
    me = lax.axis_index("dp")
    steps = [1 << bit for bit in range(count.bit_length() - 1)]
    if flip:
        steps = steps[:1] + steps[:0:-1]
    order = sorted(range(count), key=lambda piece: -(piece & 1))
    pieces = {piece: part_of(me ^ piece) for piece in order}
    for bit in steps:
        pairs = [(device, device ^ bit) for device in range(count)]
        arrived = {
            piece ^ bit: lax.ppermute(pieces[piece].astype(BF16), "dp", pairs) for piece in pieces if piece & bit
        }
        pieces = {piece: pieces[piece] + arrived[piece].astype(F32) for piece in arrived}
    return pieces[0]


def shards(frames, lengths, expert_ids, conv_kernel, conv_gain, ffn_gain, w_in, w_out, out_grad):
    utt_count = lengths.shape[0]
    frame_count, width = frames.shape
    utt_len = frame_count // utt_count
    expert_count = lax.axis_size("expert")
    capacity = max(8, 8 * (9 * frame_count // (64 * expert_count)))
    slot_total = expert_count * capacity
    taps = conv_kernel.shape[0]
    gain = conv_gain.reshape(1, width)
    ffn = ffn_gain.reshape(1, width)

    live_flat = (jnp.arange(utt_len, dtype=jnp.int32)[None, :] < lengths[:, None]).reshape(frame_count)
    target = jnp.where(live_flat, expert_ids[:, 0], expert_count)
    one_hot = (target[:, None] == jnp.arange(expert_count, dtype=jnp.int32)[None, :]).astype(jnp.int32)
    rank_in = jnp.sum((jnp.cumsum(one_hot, axis=0, dtype=jnp.int32) - 1) * one_hot, axis=1)
    dest_slot = jnp.where(live_flat, target * capacity + rank_in, slot_total)
    placing = (jnp.arange(slot_total, dtype=jnp.int32)[:, None] == dest_slot[None, :]).astype(BF16)

    send_grad = jnp.dot(placing, out_grad, preferred_element_type=F32).astype(BF16)
    grad_rows = exchange(send_grad)
    residual, conv_out, expert_in = conv_forward(frames, lengths, conv_kernel, gain, ffn)
    send_in = jnp.dot(placing, expert_in, preferred_element_type=F32).astype(BF16)
    send_in, grad_rows = lax.optimization_barrier((send_in, grad_rows))
    routed_in = exchange(send_in)
    weights_in = w_in[0]
    weights_out = w_out[0]
    hidden_grad = times_transpose(grad_rows, weights_out)
    pre_act = jnp.dot(routed_in, weights_in, preferred_element_type=F32)
    hidden = jax.nn.silu(pre_act).astype(BF16)
    pre_grad = (hidden_grad * silu_slope(pre_act)).astype(BF16)
    back_rows = times_transpose(pre_grad, weights_in).astype(BF16)
    ret_back = exchange(back_rows)
    pre_grad, back_rows = lax.optimization_barrier((pre_grad, back_rows))
    part = w_in.shape[2] // lax.axis_size("dp")
    grad_in = sum_over_dp(lambda place: contract_rows(routed_in, column_part(pre_grad, place, part)), False)
    grad_out = sum_over_dp(lambda place: contract_rows(column_part(hidden, place, part), grad_rows), True)
    out_rows = jnp.dot(hidden, weights_out, preferred_element_type=F32).astype(BF16)
    ret_out = exchange(out_rows)

    expert_back = contract_rows(placing, ret_back).astype(BF16)
    frames_grad, sums = conv_backward(
        frames, lengths, conv_kernel, gain, ffn, residual, conv_out, expert_back, out_grad
    )
    block_out = (residual + contract_rows(placing, ret_out)).astype(BF16)
    kernel_grad, gain_grads = lax.psum((sums[:taps], sums[taps:]), ("dp", "expert"))
    return (block_out, frames_grad, grad_in[None], grad_out[None], kernel_grad, gain_grads)


def solution(mesh):
    return jax.shard_map(
        shards,
        mesh=mesh,
        in_specs=(
            P(("dp", "expert"), None),
            P(("dp", "expert")),
            P(("dp", "expert"), None),
            P(),
            P(),
            P(),
            P("expert", None, None),
            P("expert", None, None),
            P(("dp", "expert"), None),
        ),
        out_specs=(
            P(("dp", "expert"), None),
            P(("dp", "expert"), None),
            P("expert", None, "dp"),
            P("expert", "dp", None),
            P(),
            P(),
        ),
        check_vma=False,
    )
```
